512 devices in a mesh: pair: 8 (over z_hi, x), row: 8 (over y, core), col: 8 (over z_lo).
Axes of the slice: x: 4, y: 4, z: 16 (z_hi: 2, z_lo: 8; z = z_hi * 8 + z_lo), core: 2. Of those that a mesh axis runs over, the one named last changes fastest.
Arguments:
- pair_elements: bfloat16 [16384, 8192], P('pair', ('row', 'col')), may hold values from -0.25 to 0.25
- valence_of: int32 [16384], P('pair'), may hold values from 0 to 1999
- conduction_of: int32 [16384], P('pair'), may hold values from 0 to 4095
- valence_depth: float32 [2000], replicated, may hold values from 0.2 to 12
- conduction_height: float32 [4096], replicated, may hold values from 0.2 to 12
Outputs:
- chi_zero: float32 [8, 1024, 8, 1024], P('row', 'pair', None, 'col')
The draws below stay inside these ranges and needn't reach their ends.
All inputs are finite; a program needn't handle non-finite values.
Results may differ from the reference program's by a relative error of at most 0.0021.
Values may be sent and summed in bfloat16 or wider, within the bound.
No kernel may reach another device: no remote copies, remote signals or barrier semaphores. Data moves between devices by JAX's collectives and lax.ppermute only.
A program may use at most 64 MiB of HBM per device.

```python
import math
import jax
import jax.numpy as jnp
from jax import lax

NG = 8192
NV = 2000
NC = 4096
PAIRS = 16384
N_ROW = 8


def place_ends(array, key, smallest, high):
    spot = [jax.random.randint(jax.random.fold_in(key, axis), (), 0, length) for axis, length in enumerate(array.shape)]
    longest = array.shape.index(max(array.shape))
    beside = spot[:longest] + [(spot[longest] + 1) % array.shape[longest]] + spot[longest + 1:]
    return array.at[tuple(spot)].set(smallest).at[tuple(beside)].set(high)


def strengthened(entries, rng, source, target, parts, factor):
    def block_of(position):
        return (jnp.arange(entries.shape[position]) // (entries.shape[position] // parts)).reshape((-1,) + (1,) * (entries.ndim - 1 - position))

    near = jax.random.permutation(rng, parts)[block_of(target)]
    other_side = (block_of(target) + parts // 2) % parts
    return jnp.where((block_of(source) == near) | (block_of(source) == other_side), factor * entries, entries)


def steps_of(key, shape, cuts, least, largest):
    def one(axis_at, parts):
        steps = jax.random.uniform(jax.random.fold_in(jax.random.fold_in(key, 6), axis_at), (parts,), jnp.float32, least / len(cuts), largest / len(cuts))
        return jnp.repeat(jnp.exp(steps), shape[axis_at] // parts).reshape((-1,) + (1,) * (len(shape) - axis_at - 1))

    gain = one(*cuts[0])
    for cut in cuts[1:]:
        gain = gain * one(*cut)
    return gain


def heavy_noise(own_key, shape, scale, limit, split, heavy, kind=jnp.bfloat16):
    result = scale * jax.random.normal(own_key, shape, jnp.float32)
    if split:
        result = result * steps_of(own_key, shape, split, -0.22, 0.18)
    return jnp.clip(strengthened(result, jax.random.fold_in(own_key, 3), *heavy), -limit, limit).astype(kind)


def setup_inputs(seed: int = 0) -> dict:
    key_list = jax.random.split(jax.random.key(seed), 6)
    return {
        "pair_elements": heavy_noise(key_list[0], (PAIRS, NG), (2 * PAIRS ** -0.5), 0.25, ((0, 8), (1, 64)), (0, 1, 64, 4.0)),
        "valence_of": place_ends(jax.random.randint(key_list[1], (PAIRS,), 0, NV), jax.random.fold_in(key_list[1], 1), 0, NV - 1).astype(jnp.int32),
        "conduction_of": place_ends(jax.random.randint(key_list[2], (PAIRS,), 0, NC), jax.random.fold_in(key_list[2], 1), 0, NC - 1).astype(jnp.int32),
        "valence_depth": jnp.clip(jnp.exp(jax.random.uniform(key_list[3], (NV,), jnp.float32, math.log(0.2), math.log(12.0))), 0.2, 12.0),
        "conduction_height": jnp.clip(jnp.exp(jax.random.uniform(key_list[4], (NC,), jnp.float32, math.log(0.2), math.log(12.0))), 0.2, 12.0),
    }


def reference(pair_elements, valence_of, conduction_of, valence_depth, conduction_height):
    pair_gap = valence_depth[valence_of] + conduction_height[conduction_of]
    factor = -4.0 / pair_gap
    weighted = (pair_elements.astype(jnp.float32) * factor[:, None]).astype(jnp.bfloat16)
    chi = lax.dot_general(weighted.astype(jnp.float32), pair_elements.astype(jnp.float32),
                          (((0,), (0,)), ((), ())), preferred_element_type=jnp.float32)
    return chi.reshape(N_ROW, NG // N_ROW, N_ROW, NG // N_ROW)
```

```python
import jax
import jax.numpy as jnp
from jax import lax
from jax.sharding import Mesh, PartitionSpec as P

NAMES = ("zh", "x", "y", "core", "zl")
SHAPE = (2, 4, 4, 2, 8)


def shift(n, s):
    return [(i, (i + s) % n) for i in range(n)]


SWAP = shift(2, 1)


def lookup(indices, table):
    hits = indices[:, None] == jnp.arange(table.shape[0], dtype=jnp.int32)[None, :]
    return jnp.sum(jnp.where(hits, table[None, :], jnp.float32(0.0)), axis=1)


def body(pair_elements, valence_of, conduction_of, valence_depth, conduction_height):
    n_pair, n_g = pair_elements.shape
    n_y, n_x, n_z = (lax.axis_size(name) for name in ("y", "x", "zl"))
    rows = lax.all_gather(pair_elements.T, "zl", axis=0, tiled=True)

    near = [pair_elements] + [
        lax.ppermute(pair_elements, "y", shift(n_y, -s)) for s in range(1, n_y)
    ]
    panels = []
    for piece in near:
        panels += [piece, lax.ppermute(piece, "core", SWAP)]
    columns = jnp.concatenate(panels, axis=1)

    pair_gap = lookup(valence_of, valence_depth) + lookup(conduction_of, conduction_height)
    factor = -4.0 / pair_gap
    weighted = (rows.astype(jnp.float32) * factor[None, :]).astype(jnp.bfloat16)
    partial = lax.dot_general(
        weighted, columns, (((1,), (0,)), ((), ())), preferred_element_type=jnp.float32
    ).astype(jnp.bfloat16)

    partial = partial.reshape(2, n_x, n_g, -1).swapaxes(0, 1)
    taken = lax.all_to_all(partial, "x", 0, 0, tiled=True)
    taken = jnp.sum(taken.astype(jnp.float32), axis=0)
    half = lax.axis_index("zh")
    kept = lax.dynamic_index_in_dim(taken, half, 0, keepdims=False)
    given = lax.dynamic_index_in_dim(taken, 1 - half, 0, keepdims=False)
    got = lax.ppermute(given.astype(jnp.bfloat16), "zh", SWAP)
    total = kept + got.astype(jnp.float32)

    total = total.reshape(n_g, n_y, 2, n_g)
    total = jnp.where(lax.axis_index("core") == 0, total, total[:, :, ::-1])
    total = jnp.concatenate([total, total], axis=1)
    total = lax.dynamic_slice_in_dim(total, lax.rem(n_y - lax.axis_index("y"), n_y), n_y, 1)
    return total.reshape(1, n_g, 2 * n_y, n_g)


def solution(mesh):
    fine = Mesh(mesh.devices.reshape(SHAPE), NAMES)
    pair, row = ("zh", "x"), ("y", "core")
    placed = (P(pair, row + ("zl",)), P(pair), P(pair), P(), P())
    return jax.shard_map(
        body, mesh=fine, in_specs=placed, out_specs=P(row, pair, None, "zl"), check_vma=False
    )
```

```python
import jax
import jax.numpy as jnp
from jax import lax
from jax.sharding import Mesh, PartitionSpec as P

NAMES = ("zh", "x", "y", "core", "zq", "zr")
SHAPE = (2, 4, 4, 2, 2, 4)


def shift(n, s):
    return [(i, (i + s) % n) for i in range(n)]


SWAP = shift(2, 1)


def lookup(indices, table):
    hits = indices[:, None] == jnp.arange(table.shape[0], dtype=jnp.int32)[None, :]
    return jnp.sum(jnp.where(hits, table[None, :], jnp.float32(0.0)), axis=1)


def panel(piece):
    n_y = lax.axis_size("y")
    near = [piece] + [lax.ppermute(piece, "y", shift(n_y, -s)) for s in range(1, n_y)]
    pieces = []
    for one in near:
        pieces += [one, lax.ppermute(one, "core", SWAP)]
    return jnp.concatenate(pieces, axis=1)


def body(pair_elements, valence_of, conduction_of, valence_depth, conduction_height):
    n_g = pair_elements.shape[1]
    n_x, n_y = lax.axis_size("x"), lax.axis_size("y")
    my_x = lax.axis_index("x")
    rows = lax.all_gather(pair_elements.T, "zr", axis=0, tiled=True)
    across = lax.ppermute(pair_elements, "zq", SWAP)
    own_columns = panel(pair_elements)
    cross_columns = panel(across)

    pair_gap = lookup(valence_of, valence_depth) + lookup(conduction_of, conduction_height)
    factor = -4.0 / pair_gap
    weighted = (rows.astype(jnp.float32) * factor[None, :]).astype(jnp.bfloat16)

    def summed_over_x(columns, earlier=None):
        partial = lax.dot_general(
            weighted, columns, (((1,), (0,)), ((), ())), preferred_element_type=jnp.float32
        ).reshape(n_x, n_g, -1)
        taken = lax.all_to_all(partial.astype(jnp.bfloat16), "x", 0, 0, tiled=True)
        if earlier is not None:
            taken, earlier = lax.optimization_barrier((taken, earlier))
        mine = jnp.arange(n_x)[:, None, None] == my_x
        others = jnp.sum(jnp.where(mine, 0.0, taken.astype(jnp.float32)), axis=0)
        return lax.dynamic_index_in_dim(partial, my_x, 0, keepdims=False) + others, earlier

    half = ("zh", "zq")
    own, _ = summed_over_x(own_columns)
    own_got = lax.ppermute(own.astype(jnp.bfloat16), half, [(2, 0), (1, 3)])
    cross, own_got = summed_over_x(cross_columns, own_got)
    cross = cross.astype(jnp.bfloat16)
    near_got = lax.ppermute(cross, half, [(0, 1), (3, 2)])
    next_got = lax.ppermute(cross, half, [(2, 1), (1, 2)])
    stays = lax.axis_index("zh") == lax.axis_index("zq")
    total = jnp.where(
        stays,
        own + own_got.astype(jnp.float32),
        near_got.astype(jnp.float32) + next_got.astype(jnp.float32),
    )

    total = total.reshape(n_g, n_y, 2, n_g)
    total = jnp.where(lax.axis_index("core") == 0, total, total[:, :, ::-1])
    total = jnp.concatenate([total, total], axis=1)
    total = lax.dynamic_slice_in_dim(total, lax.rem(n_y - lax.axis_index("y"), n_y), n_y, 1)
    return total.reshape(1, n_g, 2 * n_y, n_g)


def solution(mesh):
    fine = Mesh(mesh.devices.reshape(SHAPE), NAMES)
    pair, row, col = ("zh", "x"), ("y", "core"), ("zq", "zr")
    placed = (P(pair, row + col), P(pair), P(pair), P(), P())
    return jax.shard_map(
        body, mesh=fine, in_specs=placed, out_specs=P(row, pair, None, col), check_vma=False
    )
```

```python
import jax
import jax.numpy as jnp
from jax import lax
from jax.sharding import Mesh, PartitionSpec as P

NAMES = ("zh", "x", "y", "core", "zl")
SHAPE = (2, 4, 4, 2, 8)


def shift(n, s):
    return [(i, (i + s) % n) for i in range(n)]


def circle(n):
    return list(range(0, n, 2)) + list(range(n - 1, 0, -2))


def lookup(indices, table):
    hits = indices[:, None] == jnp.arange(table.shape[0], dtype=jnp.int32)[None, :]
    return jnp.sum(jnp.where(hits, table[None, :], jnp.float32(0.0)), axis=1)


def place(col, n):
    return jnp.where(col % 2 == 0, col // 2, (2 * n - 1 - col) // 2)


def body(pair_elements, valence_of, conduction_of, valence_depth, conduction_height):
    n_pair, n_g = pair_elements.shape
    n_x, n_z = lax.axis_size("x"), lax.axis_size("zl")
    columns = lax.all_gather(pair_elements, ("y", "core"), axis=1, tiled=True)

    order = circle(n_z)
    step = [(order[i], order[(i + 1) % n_z]) for i in range(n_z)]
    chunks = [pair_elements[: n_pair // 2], pair_elements[n_pair // 2 :]]
    arrived = [[chunk] for chunk in chunks]
    for _ in range(n_z - 1):
        for i in range(2):
            chunks[i] = lax.ppermute(chunks[i], "zl", step)
            arrived[i].append(chunks[i])
    rows = jnp.concatenate([jnp.concatenate(one, axis=1) for one in arrived], axis=0)

    pair_gap = lookup(valence_of, valence_depth) + lookup(conduction_of, conduction_height)
    factor = -4.0 / pair_gap
    weighted = (rows.astype(jnp.float32) * factor[:, None]).astype(jnp.bfloat16)

    my_half, my_x = lax.axis_index("zh"), lax.axis_index("x")
    mine_at = place(lax.axis_index("zl"), n_z)

    def summed_over_x(part, *earlier):
        partial = lax.dot_general(
            weighted, part, (((0,), (0,)), ((), ())), preferred_element_type=jnp.float32
        ).reshape(n_z, n_g, -1)

        def blocks(x):
            picked = []
            for half in (my_half, 1 - my_half):
                turn = lax.rem(mine_at - place(half * n_x + x, n_z) + n_z, n_z)
                picked.append(lax.dynamic_slice_in_dim(partial, turn, 1, 0))
            return jnp.concatenate(picked, axis=0)

        sent = [blocks(lax.rem(my_x + s, n_x)).astype(jnp.bfloat16) for s in range(1, n_x)]
        mine, *sent = lax.optimization_barrier((blocks(my_x), *sent))
        got = [lax.ppermute(one, "x", shift(n_x, s)) for s, one in enumerate(sent, 1)]
        got, earlier = lax.optimization_barrier((got, earlier))
        total = mine
        for one in got:
            total = total + one.astype(jnp.float32)
        return total[0], total[1].astype(jnp.bfloat16), *earlier

    def swapped(given):
        return lax.ppermute(given, "zh", shift(2, 1))

    width = columns.shape[1] // 2
    kept_a, given = summed_over_x(columns[:, :width])
    got_a = swapped(given)
    kept_b, given, got_a = summed_over_x(columns[:, width:], got_a)
    got_b = swapped(given)
    total_a = kept_a + got_a.astype(jnp.float32)
    total_b = kept_b + got_b.astype(jnp.float32)
    total = jnp.concatenate([total_a, total_b], axis=1)
    return total.reshape(1, n_g, -1, n_g)


def solution(mesh):
    fine = Mesh(mesh.devices.reshape(SHAPE), NAMES)
    pair, row = ("zh", "x"), ("y", "core")
    placed = (P(pair, row + ("zl",)), P(pair), P(pair), P(), P())
    return jax.shard_map(
        body, mesh=fine, in_specs=placed, out_specs=P(row, pair, None, "zl"), check_vma=False
    )
```

```python
import jax
import jax.numpy as jnp
from jax import lax
from jax.sharding import Mesh, PartitionSpec as P

NAMES = ("zh", "x", "y", "core", "zq", "zr")
SHAPE = (2, 4, 4, 2, 2, 4)


def shift(n, s):
    return [(i, (i + s) % n) for i in range(n)]


def circle(n):
    return list(range(0, n, 2)) + list(range(n - 1, 0, -2))


def place(col, n):
    return jnp.where(col % 2 == 0, col // 2, (2 * n - 1 - col) // 2)


def lookup(indices, table):
    hits = indices[:, None] == jnp.arange(table.shape[0], dtype=jnp.int32)[None, :]
    return jnp.sum(jnp.where(hits, table[None, :], jnp.float32(0.0)), axis=1)


def body(pair_elements, valence_of, conduction_of, valence_depth, conduction_height):
    n_g = pair_elements.shape[1]
    n_x, n_r = lax.axis_size("x"), lax.axis_size("zr")
    my_x = lax.axis_index("x")

    def row_panel(elements):
        return lax.all_gather(elements, ("y", "core"), axis=1, tiled=True)

    across = lax.ppermute(pair_elements, "zq", shift(2, 1))
    own_columns = row_panel(pair_elements)
    order = circle(n_r)
    step = [(order[i], order[(i + 1) % n_r]) for i in range(n_r)]
    pair_gap = lookup(valence_of, valence_depth) + lookup(conduction_of, conduction_height)
    factor = -4.0 / pair_gap
    arrived = [pair_elements]
    for _ in range(n_r - 1):
        last, factor = lax.optimization_barrier((arrived[-1], factor)) if arrived[1:] else (pair_elements, factor)
        arrived.append(lax.ppermute(last, "zr", step))
    across, _ = lax.optimization_barrier((across, arrived[n_r - 2]))
    cross_columns = row_panel(across)
    rows = lax.optimization_barrier(jnp.concatenate(arrived, axis=1))
    weighted = (rows.astype(jnp.float32) * factor[:, None]).astype(jnp.bfloat16)
    mine_at = place(lax.axis_index("zr"), n_r)

    def summed_over_x(columns, *earlier):
        partial = lax.dot_general(
            weighted, columns, (((0,), (0,)), ((), ())), preferred_element_type=jnp.float32
        ).reshape(n_r, n_g, -1)

        def block(x):
            turn = lax.rem(mine_at - place(x, n_r) + n_r, n_r)
            return lax.dynamic_index_in_dim(partial, turn, 0, keepdims=False)

        sent = [block(lax.rem(my_x + s, n_x)).astype(jnp.bfloat16) for s in range(1, n_x)]
        mine, *sent = lax.optimization_barrier((block(my_x), *sent))
        got = [lax.ppermute(one, "x", shift(n_x, s)) for s, one in enumerate(sent, 1)]
        got, earlier = lax.optimization_barrier((got, earlier))
        total = mine
        for one in got:
            total = total + one.astype(jnp.float32)
        return total, sent[0], *earlier

    half = ("zh", "zq")
    own, sent = summed_over_x(own_columns)
    cross_columns, _ = lax.optimization_barrier((cross_columns, sent))
    own_got = lax.ppermute(own.astype(jnp.bfloat16), half, [(2, 0), (1, 3)])
    cross, _, own_got = summed_over_x(cross_columns, own_got)
    cross = cross.astype(jnp.bfloat16)
    near = lax.ppermute(cross, half, [(0, 1), (3, 2)])
    far = lax.ppermute(cross, half, [(2, 1), (1, 2)])
    total = jnp.where(
        lax.axis_index("zh") == lax.axis_index("zq"),
        own + own_got.astype(jnp.float32),
        near.astype(jnp.float32) + far.astype(jnp.float32),
    )
    return total.reshape(1, n_g, -1, n_g)


def solution(mesh):
    fine = Mesh(mesh.devices.reshape(SHAPE), NAMES)
    pair, row, col = ("zh", "x"), ("y", "core"), ("zq", "zr")
    placed = (P(pair, row + col), P(pair), P(pair), P(), P())
    return jax.shard_map(
        body, mesh=fine, in_specs=placed, out_specs=P(row, pair, None, col), check_vma=False
    )
```

```python
import jax
import jax.numpy as jnp
from jax import lax
from jax.sharding import Mesh, PartitionSpec as P

NAMES = ("zh", "x", "y", "core", "zl")
SHAPE = (2, 4, 4, 2, 8)


def shift(n, s):
    return [(i, (i + s) % n) for i in range(n)]


def circle(n):
    return list(range(0, n, 2)) + list(range(n - 1, 0, -2))


def cut(array, parts):
    tiles = array.shape[0] // 16
    ends = [16 * (tiles * i // parts) for i in range(parts + 1)]
    return [array[a:b] for a, b in zip(ends, ends[1:])]


def lookup(indices, table):
    hits = indices[:, None] == jnp.arange(table.shape[0], dtype=jnp.int32)[None, :]
    return jnp.sum(jnp.where(hits, table[None, :], jnp.float32(0.0)), axis=1)


def place(col, n):
    return jnp.where(col % 2 == 0, col // 2, (2 * n - 1 - col) // 2)


def body(pair_elements, valence_of, conduction_of, valence_depth, conduction_height):
    n_pair, n_g = pair_elements.shape
    n_x, n_z = lax.axis_size("x"), lax.axis_size("zl")
    columns = lax.all_gather(pair_elements, ("y", "core"), axis=1, tiled=True)

    order = circle(n_z)
    step = [(order[i], order[(i + 1) % n_z]) for i in range(n_z)]
    chunks = cut(pair_elements, 3)
    arrived = [[chunk] for chunk in chunks]
    for _ in range(n_z - 1):
        for i in range(len(chunks)):
            chunks[i] = lax.ppermute(chunks[i], "zl", step)
            arrived[i].append(chunks[i])
    rows = jnp.concatenate([jnp.concatenate(one, axis=1) for one in arrived], axis=0)

    pair_gap = lookup(valence_of, valence_depth) + lookup(conduction_of, conduction_height)
    factor = -4.0 / pair_gap
    weighted = (rows.astype(jnp.float32) * factor[:, None]).astype(jnp.bfloat16)

    my_half, my_x = lax.axis_index("zh"), lax.axis_index("x")
    mine_at = place(lax.axis_index("zl"), n_z)

    partial = lax.dot_general(
        weighted, columns, (((0,), (0,)), ((), ())), preferred_element_type=jnp.float32
    ).reshape(n_z, n_g, -1)

    def blocks(half):
        own, *others = [
            lax.dynamic_index_in_dim(partial, turn, 0, keepdims=False)
            for turn in (
                lax.rem(mine_at - place(half * n_x + lax.rem(my_x + s, n_x), n_z) + n_z, n_z)
                for s in range(n_x)
            )
        ]
        return own, [one.astype(jnp.bfloat16) for one in others]

    def over_x(sent):
        return [lax.ppermute(one, "x", shift(n_x, s)) for s, one in enumerate(sent, 1)]

    def added(own, got):
        for one in got:
            own = own + one.astype(jnp.float32)
        return own

    given, given_sent = blocks(1 - my_half)
    kept, kept_sent = blocks(my_half)
    given, given_sent, kept, kept_sent = lax.optimization_barrier(
        (given, given_sent, kept, kept_sent)
    )
    given = added(given, over_x(given_sent)).astype(jnp.bfloat16)
    given, kept_sent = lax.optimization_barrier((given, kept_sent))
    got = lax.ppermute(given, "zh", shift(2, 1))
    total = added(kept, over_x(kept_sent)) + got.astype(jnp.float32)
    return total.reshape(1, n_g, -1, n_g)


def solution(mesh):
    fine = Mesh(mesh.devices.reshape(SHAPE), NAMES)
    pair, row = ("zh", "x"), ("y", "core")
    placed = (P(pair, row + ("zl",)), P(pair), P(pair), P(), P())
    return jax.shard_map(
        body, mesh=fine, in_specs=placed, out_specs=P(row, pair, None, "zl"), check_vma=False
    )
```

```python
import jax
import jax.numpy as jnp
from jax import lax
from jax.sharding import Mesh, PartitionSpec as P

NAMES = ("zh", "x", "y", "core", "zl")
SHAPE = (2, 4, 4, 2, 8)


def shift(n, s):
    return [(i, (i + s) % n) for i in range(n)]


def circle(n):
    return list(range(0, n, 2)) + list(range(n - 1, 0, -2))


def cut(array, parts):
    tiles = array.shape[0] // 16
    ends = [16 * (tiles * i // parts) for i in range(parts + 1)]
    return [array[a:b] for a, b in zip(ends, ends[1:])]


def lookup(indices, table):
    width = 64
    lines = -(-table.shape[0] // width)
    grid = jnp.pad(table, (0, lines * width - table.shape[0])).reshape(lines, width)
    high = lax.reduce_precision(grid, 8, 7)
    middle = lax.reduce_precision(grid - high, 8, 7)
    parts = jnp.concatenate([high, middle, grid - high - middle], axis=1).astype(jnp.bfloat16)
    column = indices[:, None]
    line_hits = (column // width == jnp.arange(lines, dtype=jnp.int32)).astype(jnp.bfloat16)
    picked = jnp.dot(line_hits, parts, preferred_element_type=jnp.float32)
    hits = column % width == jnp.arange(3 * width, dtype=jnp.int32) % width
    return jnp.sum(jnp.where(hits, picked, 0.0), axis=1, keepdims=True)


def place(col, n):
    return jnp.where(col % 2 == 0, col // 2, (2 * n - 1 - col) // 2)


def body(pair_elements, valence_of, conduction_of, valence_depth, conduction_height):
    n_pair, n_g = pair_elements.shape
    n_x, n_z = lax.axis_size("x"), lax.axis_size("zl")
    columns = lax.all_gather(pair_elements, ("y", "core"), axis=1, tiled=True)

    order = circle(n_z)
    step = [(order[i], order[(i + 1) % n_z]) for i in range(n_z)]
    chunks = list(lax.optimization_barrier(cut(pair_elements, 3)))
    arrived = [[chunk] for chunk in chunks]
    for _ in range(n_z - 1):
        for i in range(len(chunks)):
            chunks[i] = lax.ppermute(chunks[i], "zl", step)
            arrived[i].append(chunks[i])
    pair_gap = lookup(valence_of, valence_depth) + lookup(conduction_of, conduction_height)
    factors = cut(lax.optimization_barrier(-4.0 / pair_gap), len(chunks))

    def weighted(one, factor):
        return (one.astype(jnp.float32) * factor).astype(jnp.bfloat16)

    rows = jnp.zeros((n_pair, n_z * n_g), jnp.bfloat16)
    for turn in range(n_z):
        first = 0
        for pieces, factor in zip(arrived, factors):
            piece = weighted(pieces[turn], factor)
            rows = lax.dynamic_update_slice(rows, piece, (first, turn * n_g))
            first += piece.shape[0]
    rows = lax.optimization_barrier(rows)

    my_half, my_x = lax.axis_index("zh"), lax.axis_index("x")
    mine_at = place(lax.axis_index("zl"), n_z)

    partial = lax.dot_general(
        rows, columns, (((0,), (0,)), ((), ())), preferred_element_type=jnp.float32
    ).reshape(n_z, n_g, -1)

    def blocks(half):
        own, *others = [
            lax.dynamic_index_in_dim(partial, turn, 0, keepdims=False)
            for turn in (
                lax.rem(mine_at - place(half * n_x + lax.rem(my_x + s, n_x), n_z) + n_z, n_z)
                for s in range(n_x)
            )
        ]
        return own, [one.astype(jnp.bfloat16) for one in others]

    def over_x(sent):
        return [lax.ppermute(one, "x", shift(n_x, s)) for s, one in enumerate(sent, 1)]

    def added(own, got):
        for one in got:
            own = own + one.astype(jnp.float32)
        return own

    given, given_sent = blocks(1 - my_half)
    kept, kept_sent = blocks(my_half)
    given, given_sent, kept, kept_sent = lax.optimization_barrier(
        (given, given_sent, kept, kept_sent)
    )
    given = added(given, over_x(given_sent)).astype(jnp.bfloat16)
    given, kept_sent = lax.optimization_barrier((given, kept_sent))
    got = lax.ppermute(given, "zh", shift(2, 1)).astype(jnp.float32)
    total = added(kept + got, over_x(kept_sent))
    return total.reshape(1, n_g, -1, n_g)


def solution(mesh):
    fine = Mesh(mesh.devices.reshape(SHAPE), NAMES)
    pair, row = ("zh", "x"), ("y", "core")
    placed = (P(pair, row + ("zl",)), P(pair), P(pair), P(), P())
    return jax.shard_map(
        body, mesh=fine, in_specs=placed, out_specs=P(row, pair, None, "zl"), check_vma=False
    )
```

```python
import functools

import jax
import jax.numpy as jnp
from jax import lax
from jax.experimental import pallas as pl
from jax.experimental.pallas import tpu as pltpu
from jax.sharding import Mesh, PartitionSpec as P

NAMES = ("zh", "x", "y", "core", "zl")
SHAPE = (2, 4, 4, 2, 8)
WHOLE = pl.BlockSpec(memory_space=pltpu.VMEM)


def shift(n, s):
    return [(i, (i + s) % n) for i in range(n)]


def circle(n):
    return list(range(0, n, 2)) + list(range(n - 1, 0, -2))


def place(col, n):
    return jnp.where(col % 2 == 0, col // 2, (2 * n - 1 - col) // 2)


def cuts(rows, parts):
    tiles = rows // 16
    sizes = [16 * (tiles // parts + (i < tiles % parts)) for i in range(parts)]
    return [(sum(sizes[:i]), sum(sizes[: i + 1])) for i in range(parts)]


def lookup(indices, table):
    width = 64
    lines = -(-table.shape[0] // width)
    grid = jnp.pad(table, (0, lines * width - table.shape[0])).reshape(lines, width)
    high = lax.reduce_precision(grid, 8, 7)
    middle = lax.reduce_precision(grid - high, 8, 7)
    parts = jnp.concatenate([high, middle, grid - high - middle], axis=1).astype(jnp.bfloat16)
    line = jnp.arange(lines, dtype=jnp.int32)[:, None]
    line_hits = (indices[None, :] // width == line).astype(jnp.bfloat16)
    picked = lax.dot_general(
        parts, line_hits, (((0,), (0,)), ((), ())), preferred_element_type=jnp.float32
    )
    within = jnp.arange(3 * width, dtype=jnp.int32)[:, None] % width
    return jnp.sum(jnp.where(indices[None, :] % width == within, picked, 0.0), axis=0)


def turned_kernel(elements, *chunks):
    turned = elements[...].astype(jnp.float32).T.astype(jnp.bfloat16)
    first = 0
    for chunk in chunks:
        chunk[...] = turned[first : first + chunk.shape[0]]
        first += chunk.shape[0]


def turned(elements, parts):
    n_pair, n_g = elements.shape
    return pl.pallas_call(
        turned_kernel,
        out_shape=[
            jax.ShapeDtypeStruct((b - a, n_pair), elements.dtype) for a, b in cuts(n_g, parts)
        ],
        in_specs=[WHOLE],
        out_specs=[WHOLE] * parts,
    )(elements)


def product_kernel(n_turns, parts, slots, factor, columns, *refs):
    pieces = refs[: n_turns * parts]
    own, *others, rows = refs[n_turns * parts :]
    n_g = own.shape[0]
    for turn in range(n_turns):
        slot = slots[turn]

        @pl.when(slot < 1 + len(others))
        def _():
            base = slot * n_g
            offset = 0
            for piece in pieces[turn * parts : (turn + 1) * parts]:
                size = piece.shape[0]
                at = pl.multiple_of(base + offset, 16)
                value = piece[...].astype(jnp.float32) * factor[...]
                rows[pl.ds(at, size), :] = value.astype(jnp.bfloat16)
                offset += size

    for i in range(0, 1 + len(others), 2):
        both = jnp.dot(
            rows[i * n_g : (i + 2) * n_g, :], columns[...], preferred_element_type=jnp.float32
        )
        for out, value in zip((own, *others)[i : i + 2], (both[:n_g], both[n_g:])):
            out[...] = value.astype(out.dtype)


def product(slots, factor, columns, pieces, parts, n_slots):
    n_pair, width = columns.shape
    n_turns = len(pieces) // parts
    n_g = sum(piece.shape[0] for piece in pieces[:parts])
    kinds = [jnp.float32] + [jnp.bfloat16] * (n_slots - 1)
    return pl.pallas_call(
        functools.partial(product_kernel, n_turns, parts),
        out_shape=[jax.ShapeDtypeStruct((n_g, width), kind) for kind in kinds],
        in_specs=[pl.BlockSpec(memory_space=pltpu.SMEM)] + [WHOLE] * (2 + len(pieces)),
        out_specs=[WHOLE] * n_slots,
        scratch_shapes=[pltpu.VMEM((n_slots * n_g, n_pair), jnp.bfloat16)],
        compiler_params=pltpu.CompilerParams(vmem_limit_bytes=40 * 1024 * 1024),
        cost_estimate=pl.CostEstimate(
            flops=2 * n_slots * n_g * n_pair * width,
            bytes_accessed=8 * 1024 * 1024,
            transcendentals=0,
        ),
    )(slots, factor, columns, *pieces)


def body(pair_elements, valence_of, conduction_of, valence_depth, conduction_height):
    n_pair, n_g = pair_elements.shape
    n_x, n_z = lax.axis_size("x"), lax.axis_size("zl")
    columns = lax.all_gather(pair_elements, ("y", "core"), axis=1, tiled=True)

    order = circle(n_z)
    step = [(order[i], order[(i + 1) % n_z]) for i in range(n_z)]
    parts = 2
    chunks = turned(pair_elements, parts)
    pieces = list(chunks)
    for turn in range(1, n_z):
        chunks = [lax.ppermute(chunk, "zl", step) for chunk in chunks]
        pieces += chunks
        if turn == n_z // 2 - 1:
            valence_of, conduction_of, _ = lax.optimization_barrier(
                (valence_of, conduction_of, chunks[0])
            )
            pair_gap = lookup(valence_of, valence_depth)
            pair_gap = pair_gap + lookup(conduction_of, conduction_height)
            factor = (-4.0 / pair_gap)[None, :]
        if turn == n_z - 3:
            chunks[0], factor = lax.optimization_barrier((chunks[0], factor))

    my_half, my_x = lax.axis_index("zh"), lax.axis_index("x")
    turns = jnp.arange(n_z, dtype=jnp.int32)
    origin = lax.rem(place(lax.axis_index("zl"), n_z) - turns + n_z, n_z)
    col = jnp.where(origin < n_z // 2, 2 * origin, 2 * n_z - 1 - 2 * origin)
    slot = lax.rem(col % n_x - my_x + n_x, n_x)
    stays = col // n_x == my_half

    def summed_over_x(own, others):
        got = [lax.ppermute(one, "x", shift(n_x, s)) for s, one in enumerate(others, 1)]
        for one in got:
            own = own + one.astype(jnp.float32)
        return own

    given, *given_sent = product(
        jnp.where(stays, n_x, slot), factor, columns, pieces, parts, n_x
    )
    last = jnp.where(stays, slot, n_x)
    last, given, *given_sent = lax.optimization_barrier((last, given, *given_sent))
    kept, *kept_sent = product(last, factor, columns, pieces, parts, n_x)
    given = summed_over_x(given, given_sent).astype(jnp.bfloat16)
    given, *kept_sent = lax.optimization_barrier((given, *kept_sent))
    got = lax.ppermute(given, "zh", shift(2, 1)).astype(jnp.float32)
    total = summed_over_x(kept, kept_sent) + got
    return total.reshape(1, n_g, -1, n_g)


def solution(mesh):
    fine = Mesh(mesh.devices.reshape(SHAPE), NAMES)
    pair, row = ("zh", "x"), ("y", "core")
    placed = (P(pair, row + ("zl",)), P(pair), P(pair), P(), P())
    return jax.shard_map(
        body, mesh=fine, in_specs=placed, out_specs=P(row, pair, None, "zl"), check_vma=False
    )
```

```python
import functools

import jax
import jax.numpy as jnp
from jax import lax
from jax.experimental import pallas as pl
from jax.experimental.pallas import tpu as pltpu
from jax.sharding import Mesh, PartitionSpec as P

NAMES = ("zh", "x", "y", "core", "zl")
SHAPE = (2, 4, 4, 2, 8)
WHOLE = pl.BlockSpec(memory_space=pltpu.VMEM)


def shift(n, s):
    return [(i, (i + s) % n) for i in range(n)]


def circle(n):
    return list(range(0, n, 2)) + list(range(n - 1, 0, -2))


def place(col, n):
    return jnp.where(col % 2 == 0, col // 2, (2 * n - 1 - col) // 2)


def cuts(rows, parts):
    tiles = rows // 16
    sizes = [16 * (tiles // parts + (i < tiles % parts)) for i in range(parts)]
    return [(sum(sizes[:i]), sum(sizes[: i + 1])) for i in range(parts)]


def lookup(indices, table):
    width = 64
    lines = -(-table.shape[0] // width)
    grid = jnp.pad(table, (0, lines * width - table.shape[0])).reshape(lines, width)
    high = lax.reduce_precision(grid, 8, 7)
    middle = lax.reduce_precision(grid - high, 8, 7)
    parts = jnp.concatenate([high, middle, grid - high - middle], axis=1).astype(jnp.bfloat16)
    line = jnp.arange(lines, dtype=jnp.int32)[:, None]
    line_hits = (indices[None, :] // width == line).astype(jnp.bfloat16)
    picked = lax.dot_general(
        parts, line_hits, (((0,), (0,)), ((), ())), preferred_element_type=jnp.float32
    )
    within = jnp.arange(3 * width, dtype=jnp.int32)[:, None] % width
    return jnp.sum(jnp.where(indices[None, :] % width == within, picked, 0.0), axis=0)


def turned_kernel(elements, *chunks):
    turned = elements[...].astype(jnp.float32).T.astype(jnp.bfloat16)
    first = 0
    for chunk in chunks:
        chunk[...] = turned[first : first + chunk.shape[0]]
        first += chunk.shape[0]


def turned(elements, parts):
    n_pair, n_g = elements.shape
    return pl.pallas_call(
        turned_kernel,
        out_shape=[
            jax.ShapeDtypeStruct((b - a, n_pair), elements.dtype) for a, b in cuts(n_g, parts)
        ],
        in_specs=[WHOLE],
        out_specs=[WHOLE] * parts,
    )(elements)


def product_kernel(n_turns, parts, slots, factor, columns, *refs):
    pieces = refs[: n_turns * parts]
    own, *others, rows = refs[n_turns * parts :]
    n_g = own.shape[0]
    for turn in range(n_turns):
        slot = slots[turn]

        @pl.when(slot < 1 + len(others))
        def _():
            base = slot * n_g
            offset = 0
            for piece in pieces[turn * parts : (turn + 1) * parts]:
                size = piece.shape[0]
                at = pl.multiple_of(base + offset, 16)
                value = piece[...].astype(jnp.float32) * factor[...]
                rows[pl.ds(at, size), :] = value.astype(jnp.bfloat16)
                offset += size

    for i in range(0, 1 + len(others), 2):
        both = jnp.dot(
            rows[i * n_g : (i + 2) * n_g, :], columns[...], preferred_element_type=jnp.float32
        )
        for out, value in zip((own, *others)[i : i + 2], (both[:n_g], both[n_g:])):
            out[...] = value.astype(out.dtype)


def product(slots, factor, columns, pieces, parts, n_slots):
    n_pair, width = columns.shape
    n_turns = len(pieces) // parts
    n_g = sum(piece.shape[0] for piece in pieces[:parts])
    kinds = [jnp.float32] + [jnp.bfloat16] * (n_slots - 1)
    return pl.pallas_call(
        functools.partial(product_kernel, n_turns, parts),
        out_shape=[jax.ShapeDtypeStruct((n_g, width), kind) for kind in kinds],
        in_specs=[pl.BlockSpec(memory_space=pltpu.SMEM)] + [WHOLE] * (2 + len(pieces)),
        out_specs=[WHOLE] * n_slots,
        scratch_shapes=[pltpu.VMEM((n_slots * n_g, n_pair), jnp.bfloat16)],
        compiler_params=pltpu.CompilerParams(vmem_limit_bytes=40 * 1024 * 1024),
        cost_estimate=pl.CostEstimate(
            flops=2 * n_slots * n_g * n_pair * width,
            bytes_accessed=8 * 1024 * 1024,
            transcendentals=0,
        ),
    )(slots, factor, columns, *pieces)


def arrival(row, at, n):
    return (at - row + n) % n


def early_slots(n_x, n_z):
    my_x, at = lax.axis_index("x"), place(lax.axis_index("zl"), n_z)
    turns = jnp.arange(n_z, dtype=jnp.int32)
    origin = (at - turns + n_z) % n_z
    row = jnp.where(origin < n_z // 2, 2 * origin, 2 * n_z - 1 - 2 * origin)
    slot = (row % n_x - my_x + n_x) % n_x
    early = turns < arrival(place((row + n_x) % n_z, n_z), at, n_z)
    stays = arrival(place(my_x, n_z), at, n_z) < arrival(place(my_x + n_x, n_z), at, n_z)
    return (
        jnp.where(early, slot, n_x),
        jnp.where(early, n_x, slot),
        stays == (lax.axis_index("zh") == 0),
    )


def swaps(n_x, n_z):
    order = circle(n_z)
    early, late = [], []
    for x in range(n_x):
        for col in range(n_z):
            at = order.index(col)
            turns = [arrival(order.index(half * n_x + x), at, n_z) for half in range(2)]
            first = 0 if turns[0] < turns[1] else 1
            ends = [(half * n_x + x) * n_z + col for half in range(2)]
            early.append((ends[1 - first], ends[first]))
            late.append((ends[first], ends[1 - first]))
    return early, late


def body(pair_elements, valence_of, conduction_of, valence_depth, conduction_height):
    n_pair, n_g = pair_elements.shape
    n_x, n_z = lax.axis_size("x"), lax.axis_size("zl")
    columns = lax.all_gather(pair_elements, ("y", "core"), axis=1, tiled=True)

    order = circle(n_z)
    step = [(order[i], order[(i + 1) % n_z]) for i in range(n_z)]
    parts = 2
    chunks = turned(pair_elements, parts)
    pieces = list(chunks)
    early_turns = n_z - 2
    for turn in range(1, n_z):
        if turn == early_turns + 1:
            early, *early_sent = product(
                early_slots(n_x, n_z)[0], factor, columns, pieces[: early_turns * parts], parts, n_x
            )
            chunks[0], early, *early_sent = lax.optimization_barrier(
                (chunks[0], early, *early_sent)
            )
        chunks = [lax.ppermute(chunk, "zl", step) for chunk in chunks]
        pieces += chunks
        if turn == n_z // 2 - 2:
            valence_of, conduction_of, _ = lax.optimization_barrier(
                (valence_of, conduction_of, chunks[0])
            )
            pair_gap = lookup(valence_of, valence_depth)
            pair_gap = pair_gap + lookup(conduction_of, conduction_height)
            factor = (-4.0 / pair_gap)[None, :]
        if turn == n_z - 4:
            chunks[0], factor = lax.optimization_barrier((chunks[0], factor))

    def summed_over_x(own, others, *beside):
        got = [lax.ppermute(one, "x", shift(n_x, s)) for s, one in enumerate(others, 1)]
        got, beside = lax.optimization_barrier((got, beside))
        for one in got:
            own = own + one.astype(jnp.float32)
        return own, *beside

    axes = ("zh", "x", "zl")
    first_sends, then_sends = swaps(n_x, n_z)
    late_slots, early_stays = early_slots(n_x, n_z)[1:]
    early, = summed_over_x(early, early_sent)
    early_narrow, late_slots = lax.optimization_barrier((early.astype(jnp.bfloat16), late_slots))
    got_early = lax.ppermute(early_narrow, axes, first_sends)
    late, *late_sent = product(late_slots, factor, columns, pieces, parts, n_x)
    late, got_early = summed_over_x(late, late_sent, got_early)
    got_late = lax.ppermute(late.astype(jnp.bfloat16), axes, then_sends)
    kept = jnp.where(early_stays, early, late)
    total = kept + got_early.astype(jnp.float32) + got_late.astype(jnp.float32)
    return total.reshape(1, n_g, -1, n_g)


def solution(mesh):
    fine = Mesh(mesh.devices.reshape(SHAPE), NAMES)
    pair, row = ("zh", "x"), ("y", "core")
    placed = (P(pair, row + ("zl",)), P(pair), P(pair), P(), P())
    return jax.shard_map(
        body, mesh=fine, in_specs=placed, out_specs=P(row, pair, None, "zl"), check_vma=False
    )
```

```python
import functools

import jax
import jax.numpy as jnp
from jax import lax
from jax.experimental import pallas as pl
from jax.experimental.pallas import tpu as pltpu
from jax.sharding import Mesh, PartitionSpec as P

NAMES = ("zh", "x", "y", "core", "zl")
SHAPE = (2, 4, 4, 2, 8)
WHOLE = pl.BlockSpec(memory_space=pltpu.VMEM)


def shift(n, s):
    return [(i, (i + s) % n) for i in range(n)]


def circle(n):
    return list(range(0, n, 2)) + list(range(n - 1, 0, -2))


def place(col, n):
    return jnp.where(col % 2 == 0, col // 2, (2 * n - 1 - col) // 2)


def cuts(lanes, parts):
    tiles = lanes // 128
    ends = [128 * (tiles * i // parts) for i in range(parts + 1)]
    return list(zip(ends, ends[1:]))


def lookup(indices, table):
    width = 64
    lines = -(-table.shape[0] // width)
    grid = jnp.pad(table, (0, lines * width - table.shape[0])).reshape(lines, width)
    high = lax.reduce_precision(grid, 8, 7)
    middle = lax.reduce_precision(grid - high, 8, 7)
    parts = jnp.concatenate([high, middle, grid - high - middle], axis=1).astype(jnp.bfloat16)
    line = jnp.arange(lines, dtype=jnp.int32)[:, None]
    line_hits = (indices[None, :] // width == line).astype(jnp.bfloat16)
    picked = lax.dot_general(
        parts, line_hits, (((0,), (0,)), ((), ())), preferred_element_type=jnp.float32
    )
    within = jnp.arange(3 * width, dtype=jnp.int32)[:, None] % width
    return jnp.sum(jnp.where(indices[None, :] % width == within, picked, 0.0), axis=0)


def turned_kernel(elements, *chunks):
    for chunk, (a, b) in zip(chunks, cuts(elements.shape[0], len(chunks))):
        chunk[...] = elements[a:b, :].astype(jnp.float32).T.astype(jnp.bfloat16)


def turned(elements, parts):
    n_pair, n_g = elements.shape
    return pl.pallas_call(
        turned_kernel,
        out_shape=[
            jax.ShapeDtypeStruct((n_g, b - a), elements.dtype) for a, b in cuts(n_pair, parts)
        ],
        in_specs=[WHOLE],
        out_specs=[WHOLE] * parts,
    )(elements)


def product_kernel(n_turns, parts, slots, factor, columns, *refs):
    pieces = refs[: n_turns * parts]
    own, *others, rows = refs[n_turns * parts :]
    n_g = own.shape[0]
    for turn in range(n_turns):
        slot = slots[turn]

        @pl.when(slot < 1 + len(others))
        def _():
            at = pl.multiple_of(slot * n_g, 128)
            ends = cuts(rows.shape[1], parts)
            for piece, (a, b) in zip(pieces[turn * parts : (turn + 1) * parts], ends):
                value = piece[...].astype(jnp.float32) * factor[:, a:b]
                rows[pl.ds(at, n_g), a:b] = value.astype(jnp.bfloat16)

    for i in range(0, 1 + len(others), 2):
        both = jnp.dot(
            rows[i * n_g : (i + 2) * n_g, :], columns[...], preferred_element_type=jnp.float32
        )
        for out, value in zip((own, *others)[i : i + 2], (both[:n_g], both[n_g:])):
            out[...] = value.astype(out.dtype)


def product(slots, factor, columns, pieces, parts, n_slots):
    n_pair, width = columns.shape
    n_turns = len(pieces) // parts
    n_g = pieces[0].shape[0]
    kinds = [jnp.float32] + [jnp.bfloat16] * (n_slots - 1)
    return pl.pallas_call(
        functools.partial(product_kernel, n_turns, parts),
        out_shape=[jax.ShapeDtypeStruct((n_g, width), kind) for kind in kinds],
        in_specs=[pl.BlockSpec(memory_space=pltpu.SMEM)] + [WHOLE] * (2 + len(pieces)),
        out_specs=[WHOLE] * n_slots,
        scratch_shapes=[pltpu.VMEM((n_slots * n_g, n_pair), jnp.bfloat16)],
        compiler_params=pltpu.CompilerParams(vmem_limit_bytes=40 * 1024 * 1024),
        cost_estimate=pl.CostEstimate(
            flops=2 * n_slots * n_g * n_pair * width,
            bytes_accessed=8 * 1024 * 1024,
            transcendentals=0,
        ),
    )(slots, factor, columns, *pieces)


def body(pair_elements, valence_of, conduction_of, valence_depth, conduction_height):
    n_pair, n_g = pair_elements.shape
    n_x, n_z = lax.axis_size("x"), lax.axis_size("zl")
    columns = lax.all_gather(pair_elements, ("y", "core"), axis=1, tiled=True)

    order = circle(n_z)
    step = [(order[i], order[(i + 1) % n_z]) for i in range(n_z)]
    parts = 3
    chunks = turned(pair_elements, parts)
    pieces = list(chunks)
    for turn in range(1, n_z):
        if turn == n_z - 2:
            chunks[0], factor = lax.optimization_barrier((chunks[0], factor))
        chunks = [lax.ppermute(chunk, "zl", step) for chunk in chunks]
        pieces += chunks
        if turn == n_z // 2 - 2:
            valence_of, conduction_of, _ = lax.optimization_barrier(
                (valence_of, conduction_of, chunks[0])
            )
            pair_gap = lookup(valence_of, valence_depth)
            pair_gap = pair_gap + lookup(conduction_of, conduction_height)
            factor = (-4.0 / pair_gap)[None, :]

    my_half, my_x = lax.axis_index("zh"), lax.axis_index("x")
    turns = jnp.arange(n_z, dtype=jnp.int32)
    origin = lax.rem(place(lax.axis_index("zl"), n_z) - turns + n_z, n_z)
    col = jnp.where(origin < n_z // 2, 2 * origin, 2 * n_z - 1 - 2 * origin)
    slot = lax.rem(col % n_x - my_x + n_x, n_x)
    stays = col // n_x == my_half

    def summed_over_x(own, others):
        got = [lax.ppermute(one, "x", shift(n_x, s)) for s, one in enumerate(others, 1)]
        for one in got:
            own = own + one.astype(jnp.float32)
        return own

    given, *given_sent = product(
        jnp.where(stays, n_x, slot), factor, columns, pieces, parts, n_x
    )
    last = jnp.where(stays, slot, n_x)
    last, given, *given_sent = lax.optimization_barrier((last, given, *given_sent))
    kept, *kept_sent = product(last, factor, columns, pieces, parts, n_x)
    given = summed_over_x(given, given_sent).astype(jnp.bfloat16)
    given, *kept_sent = lax.optimization_barrier((given, *kept_sent))
    got = lax.ppermute(given, "zh", shift(2, 1)).astype(jnp.float32)
    total = summed_over_x(kept, kept_sent) + got
    return total.reshape(1, n_g, -1, n_g)


def solution(mesh):
    fine = Mesh(mesh.devices.reshape(SHAPE), NAMES)
    pair, row = ("zh", "x"), ("y", "core")
    placed = (P(pair, row + ("zl",)), P(pair), P(pair), P(), P())
    return jax.shard_map(
        body, mesh=fine, in_specs=placed, out_specs=P(row, pair, None, "zl"), check_vma=False
    )
```

```python
import functools

import jax
import jax.numpy as jnp
from jax import lax
from jax.experimental import pallas as pl
from jax.experimental.pallas import tpu as pltpu
from jax.sharding import Mesh, PartitionSpec as P

NAMES = ("zh", "x", "y", "core", "zl")
SHAPE = (2, 4, 4, 2, 8)
WHOLE = pl.BlockSpec(memory_space=pltpu.VMEM)


def shift(n, s):
    return [(i, (i + s) % n) for i in range(n)]


def circle(n):
    return list(range(0, n, 2)) + list(range(n - 1, 0, -2))


def place(col, n):
    return jnp.where(col % 2 == 0, col // 2, (2 * n - 1 - col) // 2)


def cuts(lanes, parts):
    tiles = lanes // 128
    ends = [128 * (tiles * i // parts) for i in range(parts + 1)]
    return list(zip(ends, ends[1:]))


def lookup(indices, table):
    width = 64
    lines = -(-table.shape[0] // width)
    grid = jnp.pad(table, (0, lines * width - table.shape[0])).reshape(lines, width)
    high = lax.reduce_precision(grid, 8, 7)
    middle = lax.reduce_precision(grid - high, 8, 7)
    parts = jnp.concatenate([high, middle, grid - high - middle], axis=1).astype(jnp.bfloat16)
    line = jnp.arange(lines, dtype=jnp.int32)[:, None]
    line_hits = (indices[None, :] // width == line).astype(jnp.bfloat16)
    picked = lax.dot_general(
        parts, line_hits, (((0,), (0,)), ((), ())), preferred_element_type=jnp.float32
    )
    within = jnp.arange(3 * width, dtype=jnp.int32)[:, None] % width
    return jnp.sum(jnp.where(indices[None, :] % width == within, picked, 0.0), axis=0)


def turned_kernel(elements, *chunks):
    for chunk, (a, b) in zip(chunks, cuts(elements.shape[0], len(chunks))):
        chunk[...] = elements[a:b, :].astype(jnp.float32).T.astype(jnp.bfloat16)


def turned(elements, parts):
    n_pair, n_g = elements.shape
    return pl.pallas_call(
        turned_kernel,
        out_shape=[
            jax.ShapeDtypeStruct((n_g, b - a), elements.dtype) for a, b in cuts(n_pair, parts)
        ],
        in_specs=[WHOLE],
        out_specs=[WHOLE] * parts,
    )(elements)


def product_kernel(n_rows, n_turns, parts, slots, order, factor, *refs):
    near, pieces = refs[:n_rows], refs[n_rows : n_rows + n_turns * parts]
    own, *others, rows, columns = refs[n_rows + n_turns * parts :]
    n_g = own.shape[0]
    for i, piece in enumerate(near):
        at = pl.multiple_of(order[i] * n_g, 128)
        columns[:, pl.ds(at, n_g)] = piece[...]
    for turn in range(n_turns):
        slot = slots[turn]

        @pl.when(slot < 1 + len(others))
        def _():
            at = pl.multiple_of(slot * n_g, 128)
            ends = cuts(rows.shape[1], parts)
            for piece, (a, b) in zip(pieces[turn * parts : (turn + 1) * parts], ends):
                value = piece[...].astype(jnp.float32) * factor[:, a:b]
                rows[pl.ds(at, n_g), a:b] = value.astype(jnp.bfloat16)

    for i in range(0, 1 + len(others), 2):
        both = jnp.dot(
            rows[i * n_g : (i + 2) * n_g, :], columns[...], preferred_element_type=jnp.float32
        )
        for out, value in zip((own, *others)[i : i + 2], (both[:n_g], both[n_g:])):
            out[...] = value.astype(out.dtype)


def product(slots, order, factor, near, pieces, parts, n_slots):
    n_pair, n_g = near[0].shape
    width = n_g * len(near)
    n_turns = len(pieces) // parts
    kinds = [jnp.float32] + [jnp.bfloat16] * (n_slots - 1)
    return pl.pallas_call(
        functools.partial(product_kernel, len(near), n_turns, parts),
        out_shape=[jax.ShapeDtypeStruct((n_g, width), kind) for kind in kinds],
        in_specs=[pl.BlockSpec(memory_space=pltpu.SMEM)] * 2
        + [WHOLE] * (1 + len(near) + len(pieces)),
        out_specs=[WHOLE] * n_slots,
        scratch_shapes=[
            pltpu.VMEM((n_slots * n_g, n_pair), jnp.bfloat16),
            pltpu.VMEM((n_pair, width), jnp.bfloat16),
        ],
        compiler_params=pltpu.CompilerParams(vmem_limit_bytes=40 * 1024 * 1024),
        cost_estimate=pl.CostEstimate(
            flops=2 * n_slots * n_g * n_pair * width,
            bytes_accessed=8 * 1024 * 1024,
            transcendentals=0,
        ),
    )(slots, order, factor, *near, *pieces)


def body(pair_elements, valence_of, conduction_of, valence_depth, conduction_height):
    n_pair, n_g = pair_elements.shape
    n_x, n_z = lax.axis_size("x"), lax.axis_size("zl")
    n_row = lax.axis_size("y") * lax.axis_size("core")
    near = [pair_elements]

    def fetch(count, after):
        source, _ = lax.optimization_barrier((pair_elements, after))
        for s in range(len(near), min(len(near) + count, n_row)):
            near.append(lax.ppermute(source, ("y", "core"), shift(n_row, -s)))

    order = circle(n_z)
    step = [(order[i], order[(i + 1) % n_z]) for i in range(n_z)]
    parts = 3
    chunks = turned(pair_elements, parts)
    pieces = list(chunks)
    fetch(2, chunks[0])
    for turn in range(1, n_z):
        if turn >= n_z // 2:
            first = 1 + 2 * (turn - n_z // 2)
            chunks[0], *near[first : first + 2] = lax.optimization_barrier(
                (chunks[0], *near[first : first + 2])
            )
        if turn == n_z - 2:
            chunks[0], factor = lax.optimization_barrier((chunks[0], factor))
        chunks = [lax.ppermute(chunk, "zl", step) for chunk in chunks]
        pieces += chunks
        fetch(2, chunks[0])
        if turn == n_z // 2 - 2:
            valence_of, conduction_of, _ = lax.optimization_barrier(
                (valence_of, conduction_of, chunks[0])
            )
            pair_gap = lookup(valence_of, valence_depth)
            pair_gap = pair_gap + lookup(conduction_of, conduction_height)
            factor = (-4.0 / pair_gap)[None, :]

    my_row = lax.axis_index("y") * lax.axis_size("core") + lax.axis_index("core")
    places = lax.rem(my_row + jnp.arange(n_row, dtype=jnp.int32), n_row)
    my_half, my_x = lax.axis_index("zh"), lax.axis_index("x")
    turns = jnp.arange(n_z, dtype=jnp.int32)
    origin = lax.rem(place(lax.axis_index("zl"), n_z) - turns + n_z, n_z)
    col = jnp.where(origin < n_z // 2, 2 * origin, 2 * n_z - 1 - 2 * origin)
    slot = lax.rem(col % n_x - my_x + n_x, n_x)
    stays = col // n_x == my_half

    def summed_over_x(own, others):
        got = [lax.ppermute(one, "x", shift(n_x, s)) for s, one in enumerate(others, 1)]
        for one in got:
            own = own + one.astype(jnp.float32)
        return own

    given, *given_sent = product(
        jnp.where(stays, n_x, slot), places, factor, near, pieces, parts, n_x
    )
    last = jnp.where(stays, slot, n_x)
    last, given, *given_sent = lax.optimization_barrier((last, given, *given_sent))
    kept, *kept_sent = product(last, places, factor, near, pieces, parts, n_x)
    given = summed_over_x(given, given_sent).astype(jnp.bfloat16)
    given, *kept_sent = lax.optimization_barrier((given, *kept_sent))
    got = lax.ppermute(given, "zh", shift(2, 1)).astype(jnp.float32)
    total = summed_over_x(kept, kept_sent) + got
    return total.reshape(1, n_g, -1, n_g)


def solution(mesh):
    fine = Mesh(mesh.devices.reshape(SHAPE), NAMES)
    pair, row = ("zh", "x"), ("y", "core")
    placed = (P(pair, row + ("zl",)), P(pair), P(pair), P(), P())
    return jax.shard_map(
        body, mesh=fine, in_specs=placed, out_specs=P(row, pair, None, "zl"), check_vma=False
    )
```

```python
import functools

import jax
import jax.numpy as jnp
from jax import lax
from jax.experimental import pallas as pl
from jax.experimental.pallas import tpu as pltpu
from jax.sharding import Mesh, PartitionSpec as P

NAMES = ("zh", "x", "y", "core", "zl")
SHAPE = (2, 4, 4, 2, 8)
WHOLE = pl.BlockSpec(memory_space=pltpu.VMEM)


def shift(n, s):
    return [(i, (i + s) % n) for i in range(n)]


def circle(n):
    return list(range(0, n, 2)) + list(range(n - 1, 0, -2))


def place(col, n):
    return jnp.where(col % 2 == 0, col // 2, (2 * n - 1 - col) // 2)


def cuts(lanes, parts):
    tiles = lanes // 128
    ends = [128 * (tiles * i // parts) for i in range(parts + 1)]
    return list(zip(ends, ends[1:]))


def lookup(indices, table):
    width = 64
    lines = -(-table.shape[0] // width)
    grid = jnp.pad(table, (0, lines * width - table.shape[0])).reshape(lines, width)
    high = lax.reduce_precision(grid, 8, 7)
    middle = lax.reduce_precision(grid - high, 8, 7)
    parts = jnp.concatenate([high, middle, grid - high - middle], axis=1).astype(jnp.bfloat16)
    line = jnp.arange(lines, dtype=jnp.int32)[:, None]
    line_hits = (indices[None, :] // width == line).astype(jnp.bfloat16)
    picked = lax.dot_general(
        parts, line_hits, (((0,), (0,)), ((), ())), preferred_element_type=jnp.float32
    )
    within = jnp.arange(3 * width, dtype=jnp.int32)[:, None] % width
    return jnp.sum(jnp.where(indices[None, :] % width == within, picked, 0.0), axis=0)


def turned_kernel(elements, *chunks):
    for chunk, (a, b) in zip(chunks, cuts(elements.shape[0], len(chunks))):
        chunk[...] = elements[a:b, :].astype(jnp.float32).T.astype(jnp.bfloat16)


def turned(elements, parts):
    n_pair, n_g = elements.shape
    return pl.pallas_call(
        turned_kernel,
        out_shape=[
            jax.ShapeDtypeStruct((n_g, b - a), elements.dtype) for a, b in cuts(n_pair, parts)
        ],
        in_specs=[WHOLE],
        out_specs=[WHOLE] * parts,
    )(elements)


def ordered_kernel(n_g, order, *refs):
    *near, columns = refs
    for i, pair in enumerate(near):
        for core in range(2):
            at = pl.multiple_of(order[2 * i + core] * n_g, 128)
            columns[:, pl.ds(at, n_g)] = pair[:, core * n_g : (core + 1) * n_g]


def ordered(order, near):
    n_pair, width = near[0].shape
    return pl.pallas_call(
        functools.partial(ordered_kernel, width // 2),
        out_shape=jax.ShapeDtypeStruct((n_pair, width * len(near)), near[0].dtype),
        in_specs=[pl.BlockSpec(memory_space=pltpu.SMEM)] + [WHOLE] * len(near),
        out_specs=WHOLE,
        compiler_params=pltpu.CompilerParams(vmem_limit_bytes=24 * 1024 * 1024),
    )(order, *near)


def product_kernel(n_turns, parts, slots, factor, columns, *refs):
    pieces = refs[: n_turns * parts]
    own, *others, rows = refs[n_turns * parts :]
    n_g = own.shape[0]
    for turn in range(n_turns):
        slot = slots[turn]

        @pl.when(slot < 1 + len(others))
        def _():
            at = pl.multiple_of(slot * n_g, 128)
            ends = cuts(rows.shape[1], parts)
            for piece, (a, b) in zip(pieces[turn * parts : (turn + 1) * parts], ends):
                value = piece[...].astype(jnp.float32) * factor[:, a:b]
                rows[pl.ds(at, n_g), a:b] = value.astype(jnp.bfloat16)

    for i in range(0, 1 + len(others), 2):
        both = jnp.dot(
            rows[i * n_g : (i + 2) * n_g, :], columns[...], preferred_element_type=jnp.float32
        )
        for out, value in zip((own, *others)[i : i + 2], (both[:n_g], both[n_g:])):
            out[...] = value.astype(out.dtype)


def product(slots, factor, columns, pieces, parts, n_slots):
    n_pair, width = columns.shape
    n_turns = len(pieces) // parts
    n_g = pieces[0].shape[0]
    kinds = [jnp.float32] + [jnp.bfloat16] * (n_slots - 1)
    return pl.pallas_call(
        functools.partial(product_kernel, n_turns, parts),
        out_shape=[jax.ShapeDtypeStruct((n_g, width), kind) for kind in kinds],
        in_specs=[pl.BlockSpec(memory_space=pltpu.SMEM)] + [WHOLE] * (2 + len(pieces)),
        out_specs=[WHOLE] * n_slots,
        scratch_shapes=[pltpu.VMEM((n_slots * n_g, n_pair), jnp.bfloat16)],
        compiler_params=pltpu.CompilerParams(vmem_limit_bytes=24 * 1024 * 1024),
        cost_estimate=pl.CostEstimate(
            flops=2 * n_slots * n_g * n_pair * width,
            bytes_accessed=8 * 1024 * 1024,
            transcendentals=0,
        ),
    )(slots, factor, columns, *pieces)


def body(pair_elements, valence_of, conduction_of, valence_depth, conduction_height):
    n_pair, n_g = pair_elements.shape
    n_x, n_z = lax.axis_size("x"), lax.axis_size("zl")
    n_y = lax.axis_size("y")

    order = circle(n_z)
    step = [(order[i], order[(i + 1) % n_z]) for i in range(n_z)]
    parts = 2
    chunks = turned(pair_elements, parts)
    pieces = list(chunks)
    both = jnp.concatenate(
        [pair_elements, lax.ppermute(pair_elements, "core", shift(2, 1))], axis=1
    )
    near = [both] + [lax.ppermute(both, "y", shift(n_y, -s)) for s in range(1, n_y)]
    pair = jnp.arange(2 * n_y, dtype=jnp.int32)
    places = 2 * lax.rem(lax.axis_index("y") + pair // 2, n_y)
    places = places + lax.rem(lax.axis_index("core") + pair % 2, 2)
    for turn in range(1, n_z):
        if turn == 6:
            columns = ordered(places, near)
            chunks[0], columns = lax.optimization_barrier((chunks[0], columns))
        if turn == n_z - 2:
            chunks[0], factor = lax.optimization_barrier((chunks[0], factor))
        chunks = [lax.ppermute(chunk, "zl", step) for chunk in chunks]
        pieces += chunks
        if turn == n_z // 2 - 2:
            valence_of, conduction_of, _ = lax.optimization_barrier(
                (valence_of, conduction_of, chunks[0])
            )
            pair_gap = lookup(valence_of, valence_depth)
            pair_gap = pair_gap + lookup(conduction_of, conduction_height)
            factor = (-4.0 / pair_gap)[None, :]

    my_half, my_x = lax.axis_index("zh"), lax.axis_index("x")
    turns = jnp.arange(n_z, dtype=jnp.int32)
    origin = lax.rem(place(lax.axis_index("zl"), n_z) - turns + n_z, n_z)
    col = jnp.where(origin < n_z // 2, 2 * origin, 2 * n_z - 1 - 2 * origin)
    slot = lax.rem(col % n_x - my_x + n_x, n_x)
    stays = col // n_x == my_half

    def summed_over_x(own, others):
        got = [lax.ppermute(one, "x", shift(n_x, s)) for s, one in enumerate(others, 1)]
        for one in got:
            own = own + one.astype(jnp.float32)
        return own

    given, *given_sent = product(
        jnp.where(stays, n_x, slot), factor, columns, pieces, parts, n_x
    )
    last = jnp.where(stays, slot, n_x)
    last, given, *given_sent = lax.optimization_barrier((last, given, *given_sent))
    kept, *kept_sent = product(last, factor, columns, pieces, parts, n_x)
    given = summed_over_x(given, given_sent).astype(jnp.bfloat16)
    given, *kept_sent = lax.optimization_barrier((given, *kept_sent))
    got = lax.ppermute(given, "zh", shift(2, 1)).astype(jnp.float32)
    total = summed_over_x(kept, kept_sent) + got
    return total.reshape(1, n_g, -1, n_g)


def solution(mesh):
    fine = Mesh(mesh.devices.reshape(SHAPE), NAMES)
    pair, row = ("zh", "x"), ("y", "core")
    placed = (P(pair, row + ("zl",)), P(pair), P(pair), P(), P())
    return jax.shard_map(
        body, mesh=fine, in_specs=placed, out_specs=P(row, pair, None, "zl"), check_vma=False
    )
```

```python
import functools

import jax
import jax.numpy as jnp
from jax import lax
from jax.experimental import pallas as pl
from jax.experimental.pallas import tpu as pltpu
from jax.sharding import Mesh, PartitionSpec as P

NAMES = ("zh", "x", "y", "core", "zl")
SHAPE = (2, 4, 4, 2, 8)
WHOLE = pl.BlockSpec(memory_space=pltpu.VMEM)


def shift(n, s):
    return [(i, (i + s) % n) for i in range(n)]


def circle(n):
    return list(range(0, n, 2)) + list(range(n - 1, 0, -2))


def place(col, n):
    return jnp.where(col % 2 == 0, col // 2, (2 * n - 1 - col) // 2)


def cuts(rows, parts):
    tiles = rows // 16
    sizes = [16 * (tiles // parts + (i < tiles % parts)) for i in range(parts)]
    return [(sum(sizes[:i]), sum(sizes[: i + 1])) for i in range(parts)]


def lookup(indices, table):
    width = 64
    lines = -(-table.shape[0] // width)
    grid = jnp.pad(table, (0, lines * width - table.shape[0])).reshape(lines, width)
    high = lax.reduce_precision(grid, 8, 7)
    middle = lax.reduce_precision(grid - high, 8, 7)
    parts = jnp.concatenate([high, middle, grid - high - middle], axis=1).astype(jnp.bfloat16)
    line = jnp.arange(lines, dtype=jnp.int32)[:, None]
    line_hits = (indices[None, :] // width == line).astype(jnp.bfloat16)
    picked = lax.dot_general(
        parts, line_hits, (((0,), (0,)), ((), ())), preferred_element_type=jnp.float32
    )
    within = jnp.arange(3 * width, dtype=jnp.int32)[:, None] % width
    return jnp.sum(jnp.where(indices[None, :] % width == within, picked, 0.0), axis=0)


def turned_kernel(elements, *chunks):
    turned = elements[...].astype(jnp.float32).T.astype(jnp.bfloat16)
    first = 0
    for chunk in chunks:
        chunk[...] = turned[first : first + chunk.shape[0]]
        first += chunk.shape[0]


def turned(elements, parts):
    n_pair, n_g = elements.shape
    return pl.pallas_call(
        turned_kernel,
        out_shape=[
            jax.ShapeDtypeStruct((b - a, n_pair), elements.dtype) for a, b in cuts(n_g, parts)
        ],
        in_specs=[WHOLE],
        out_specs=[WHOLE] * parts,
    )(elements)


def product_kernel(n_turns, parts, slots, factor, columns, *refs):
    pieces = refs[: n_turns * parts]
    own, *others, rows = refs[n_turns * parts :]
    n_g = own.shape[0]
    for turn in range(n_turns):
        slot = slots[turn]

        @pl.when(slot < 1 + len(others))
        def _():
            base = slot * n_g
            offset = 0
            for piece in pieces[turn * parts : (turn + 1) * parts]:
                size = piece.shape[0]
                at = pl.multiple_of(base + offset, 16)
                value = piece[...].astype(jnp.float32) * factor[...]
                rows[pl.ds(at, size), :] = value.astype(jnp.bfloat16)
                offset += size

    for i in range(0, 1 + len(others), 2):
        both = jnp.dot(
            rows[i * n_g : (i + 2) * n_g, :], columns[...], preferred_element_type=jnp.float32
        )
        for out, value in zip((own, *others)[i : i + 2], (both[:n_g], both[n_g:])):
            out[...] = value.astype(out.dtype)


def product(slots, factor, columns, pieces, parts, n_slots):
    n_pair, width = columns.shape
    n_turns = len(pieces) // parts
    n_g = sum(piece.shape[0] for piece in pieces[:parts])
    kinds = [jnp.float32] + [jnp.bfloat16] * (n_slots - 1)
    return pl.pallas_call(
        functools.partial(product_kernel, n_turns, parts),
        out_shape=[jax.ShapeDtypeStruct((n_g, width), kind) for kind in kinds],
        in_specs=[pl.BlockSpec(memory_space=pltpu.SMEM)] + [WHOLE] * (2 + len(pieces)),
        out_specs=[WHOLE] * n_slots,
        scratch_shapes=[pltpu.VMEM((n_slots * n_g, n_pair), jnp.bfloat16)],
        compiler_params=pltpu.CompilerParams(vmem_limit_bytes=40 * 1024 * 1024),
        cost_estimate=pl.CostEstimate(
            flops=2 * n_slots * n_g * n_pair * width,
            bytes_accessed=8 * 1024 * 1024,
            transcendentals=0,
        ),
    )(slots, factor, columns, *pieces)


def body(pair_elements, valence_of, conduction_of, valence_depth, conduction_height):
    n_pair, n_g = pair_elements.shape
    n_x, n_z = lax.axis_size("x"), lax.axis_size("zl")
    columns = lax.all_gather(pair_elements, ("y", "core"), axis=1, tiled=True)

    order = circle(n_z)
    step = [(order[i], order[(i + 1) % n_z]) for i in range(n_z)]
    parts = 2
    chunks = turned(pair_elements, parts)
    pieces = list(chunks)
    for turn in range(1, n_z):
        chunks = [lax.ppermute(chunk, "zl", step) for chunk in chunks]
        pieces += chunks
        if turn == n_z // 2 - 1:
            valence_of, conduction_of, _ = lax.optimization_barrier(
                (valence_of, conduction_of, chunks[0])
            )
            pair_gap = lookup(valence_of, valence_depth)
            pair_gap = pair_gap + lookup(conduction_of, conduction_height)
            factor = (-4.0 / pair_gap)[None, :]
        if turn == n_z - 3:
            chunks[0], factor = lax.optimization_barrier((chunks[0], factor))

    my_half, my_x = lax.axis_index("zh"), lax.axis_index("x")
    turns = jnp.arange(n_z, dtype=jnp.int32)
    origin = lax.rem(place(lax.axis_index("zl"), n_z) - turns + n_z, n_z)
    col = jnp.where(origin < n_z // 2, 2 * origin, 2 * n_z - 1 - 2 * origin)
    slot = lax.rem(col % n_x - my_x + n_x, n_x)
    stays = col // n_x == my_half

    def summed_over_x(own, others):
        apart = sorted(range(1, n_x), key=lambda s: min(s, n_x - s))
        got = [lax.ppermute(others[s - 1], "x", shift(n_x, s)) for s in apart]
        for one in got:
            own = own + one.astype(jnp.float32)
        return own

    given, *given_sent = product(
        jnp.where(stays, n_x, slot), factor, columns, pieces, parts, n_x
    )
    last = jnp.where(stays, slot, n_x)
    last, given, *given_sent = lax.optimization_barrier((last, given, *given_sent))
    kept, *kept_sent = product(last, factor, columns, pieces, parts, n_x)
    given = summed_over_x(given, given_sent).astype(jnp.bfloat16)
    given, *kept_sent = lax.optimization_barrier((given, *kept_sent))
    got = lax.ppermute(given, "zh", shift(2, 1)).astype(jnp.float32)
    total = summed_over_x(kept, kept_sent) + got
    return total.reshape(1, n_g, -1, n_g)


def solution(mesh):
    fine = Mesh(mesh.devices.reshape(SHAPE), NAMES)
    pair, row = ("zh", "x"), ("y", "core")
    placed = (P(pair, row + ("zl",)), P(pair), P(pair), P(), P())
    return jax.shard_map(
        body, mesh=fine, in_specs=placed, out_specs=P(row, pair, None, "zl"), check_vma=False
    )
```

```python
import functools

import jax
import jax.numpy as jnp
from jax import lax
from jax.experimental import pallas as pl
from jax.experimental.pallas import tpu as pltpu
from jax.sharding import Mesh, PartitionSpec as P

NAMES = ("zh", "x", "y", "core", "zl")
SHAPE = (2, 4, 4, 2, 8)
WHOLE = pl.BlockSpec(memory_space=pltpu.VMEM)


def shift(n, s):
    return [(i, (i + s) % n) for i in range(n)]


def circle(n):
    return list(range(0, n, 2)) + list(range(n - 1, 0, -2))


def place(col, n):
    return jnp.where(col % 2 == 0, col // 2, (2 * n - 1 - col) // 2)


def cuts(rows, parts):
    tiles = rows // 16
    sizes = [16 * (tiles // parts + (i < tiles % parts)) for i in range(parts)]
    return [(sum(sizes[:i]), sum(sizes[: i + 1])) for i in range(parts)]


def lookup(indices, table):
    width = 64
    lines = -(-table.shape[0] // width)
    grid = jnp.pad(table, (0, lines * width - table.shape[0])).reshape(lines, width)
    high = lax.reduce_precision(grid, 8, 7)
    middle = lax.reduce_precision(grid - high, 8, 7)
    parts = jnp.concatenate([high, middle, grid - high - middle], axis=1).astype(jnp.bfloat16)
    line = jnp.arange(lines, dtype=jnp.int32)[:, None]
    line_hits = (indices[None, :] // width == line).astype(jnp.bfloat16)
    picked = lax.dot_general(
        parts, line_hits, (((0,), (0,)), ((), ())), preferred_element_type=jnp.float32
    )
    within = jnp.arange(3 * width, dtype=jnp.int32)[:, None] % width
    return jnp.sum(jnp.where(indices[None, :] % width == within, picked, 0.0), axis=0)


def turned_kernel(first, elements, chunk):
    value = elements[...].astype(jnp.float32).T
    chunk[...] = value[first : first + chunk.shape[0]].astype(jnp.bfloat16)


def turned(elements, parts):
    n_pair, n_g = elements.shape
    return [
        pl.pallas_call(
            functools.partial(turned_kernel, a),
            out_shape=jax.ShapeDtypeStruct((b - a, n_pair), elements.dtype),
            in_specs=[WHOLE],
            out_specs=WHOLE,
        )(elements)
        for a, b in cuts(n_g, parts)
    ]


def product_kernel(n_turns, parts, slots, factor, columns, *refs):
    pieces = refs[: n_turns * parts]
    own, *others, rows = refs[n_turns * parts :]
    n_g = own.shape[0]
    for turn in range(n_turns):
        slot = slots[turn]

        @pl.when(slot < 1 + len(others))
        def _():
            base = slot * n_g
            offset = 0
            for piece in pieces[turn * parts : (turn + 1) * parts]:
                size = piece.shape[0]
                at = pl.multiple_of(base + offset, 16)
                value = piece[...].astype(jnp.float32) * factor[...]
                rows[pl.ds(at, size), :] = value.astype(jnp.bfloat16)
                offset += size

    for i in range(0, 1 + len(others), 2):
        both = jnp.dot(
            rows[i * n_g : (i + 2) * n_g, :], columns[...], preferred_element_type=jnp.float32
        )
        for out, value in zip((own, *others)[i : i + 2], (both[:n_g], both[n_g:])):
            out[...] = value.astype(out.dtype)


def product(slots, factor, columns, pieces, parts, n_slots):
    n_pair, width = columns.shape
    n_turns = len(pieces) // parts
    n_g = sum(piece.shape[0] for piece in pieces[:parts])
    kinds = [jnp.float32] + [jnp.bfloat16] * (n_slots - 1)
    return pl.pallas_call(
        functools.partial(product_kernel, n_turns, parts),
        out_shape=[jax.ShapeDtypeStruct((n_g, width), kind) for kind in kinds],
        in_specs=[pl.BlockSpec(memory_space=pltpu.SMEM)] + [WHOLE] * (2 + len(pieces)),
        out_specs=[WHOLE] * n_slots,
        scratch_shapes=[pltpu.VMEM((n_slots * n_g, n_pair), jnp.bfloat16)],
        compiler_params=pltpu.CompilerParams(vmem_limit_bytes=40 * 1024 * 1024),
        cost_estimate=pl.CostEstimate(
            flops=2 * n_slots * n_g * n_pair * width,
            bytes_accessed=8 * 1024 * 1024,
            transcendentals=0,
        ),
    )(slots, factor, columns, *pieces)


def body(pair_elements, valence_of, conduction_of, valence_depth, conduction_height):
    n_pair, n_g = pair_elements.shape
    n_x, n_z = lax.axis_size("x"), lax.axis_size("zl")
    columns = lax.all_gather(pair_elements, ("y", "core"), axis=1, tiled=True)

    order = circle(n_z)
    step = [(order[i], order[(i + 1) % n_z]) for i in range(n_z)]
    parts = 2
    chunks = turned(pair_elements, parts)
    pieces = list(chunks)
    for turn in range(1, n_z):
        chunks = [lax.ppermute(chunk, "zl", step) for chunk in chunks]
        pieces += chunks
        if turn == n_z // 2 - 1:
            valence_of, conduction_of, _ = lax.optimization_barrier(
                (valence_of, conduction_of, chunks[0])
            )
            pair_gap = lookup(valence_of, valence_depth)
            pair_gap = pair_gap + lookup(conduction_of, conduction_height)
            factor = (-4.0 / pair_gap)[None, :]
        if turn == n_z - 3:
            chunks[0], factor = lax.optimization_barrier((chunks[0], factor))

    my_half, my_x = lax.axis_index("zh"), lax.axis_index("x")
    turns = jnp.arange(n_z, dtype=jnp.int32)
    origin = lax.rem(place(lax.axis_index("zl"), n_z) - turns + n_z, n_z)
    col = jnp.where(origin < n_z // 2, 2 * origin, 2 * n_z - 1 - 2 * origin)
    slot = lax.rem(col % n_x - my_x + n_x, n_x)
    stays = col // n_x == my_half

    def summed_over_x(own, others):
        got = [lax.ppermute(one, "x", shift(n_x, s)) for s, one in enumerate(others, 1)]
        for one in got:
            own = own + one.astype(jnp.float32)
        return own

    given, *given_sent = product(
        jnp.where(stays, n_x, slot), factor, columns, pieces, parts, n_x
    )
    last = jnp.where(stays, slot, n_x)
    last, given, *given_sent = lax.optimization_barrier((last, given, *given_sent))
    kept, *kept_sent = product(last, factor, columns, pieces, parts, n_x)
    given = summed_over_x(given, given_sent).astype(jnp.bfloat16)
    given, *kept_sent = lax.optimization_barrier((given, *kept_sent))
    got = lax.ppermute(given, "zh", shift(2, 1)).astype(jnp.float32)
    total = summed_over_x(kept, kept_sent) + got
    return total.reshape(1, n_g, -1, n_g)


def solution(mesh):
    fine = Mesh(mesh.devices.reshape(SHAPE), NAMES)
    pair, row = ("zh", "x"), ("y", "core")
    placed = (P(pair, row + ("zl",)), P(pair), P(pair), P(), P())
    return jax.shard_map(
        body, mesh=fine, in_specs=placed, out_specs=P(row, pair, None, "zl"), check_vma=False
    )
```
